32 devices in a mesh: parts: 2 (over y), wide: 4 (over x, core), narrow: 4 (over z).
Axes of the slice: x: 2, y: 2, z: 4, core: 2. Of those that a mesh axis runs over, the one named last changes fastest.
Arguments:
- cand_grads: bfloat16 [1280, 16384], P(('parts', 'wide'), 'narrow'), parts along dimension 0, may hold values from -6 to 6
- train_feats: bfloat16 [1024, 16384], P(('parts', 'wide'), 'narrow'), parts along dimension 0, may hold values from -0.046875 to 0.046875
- span_ids: int32 [1024], P('parts'), parts along dimension 0, may hold values from 0 to 63, never falling along the last dimension, each value on 1 to 32 neighbouring positions
- group_ids: int32 [1280], P(('parts', 'wide')), parts along dimension 0, may hold values from 0 to 39, as said below
- eig_values: float32 [128, 128], replicated, may hold values from 0.05 to 2
- input_basis: float32 [128, 128], replicated, may hold values from -0.5 to 0.5
- basis: float32 [128, 128], replicated, may hold values from -0.5 to 0.5
Outputs:
- doc_influence: float32 [1280, 64], P(('parts', 'wide'), 'narrow'), parts along dimension 0
The draws below stay inside these ranges and needn't reach their ends.
There are 2 independent parts, one for each index of `parts`. The reference program is written for one: setup_inputs(seed, part) draws one part's arguments, and reference() takes and returns one part's arrays. A program takes and returns all parts, laid end to end along the dimension named above; an argument that names none is the same for every part. Nothing has to cross between parts.
Inputs may be any that keep to these rules, and one draw needn't show every extreme that they name: `group_ids`: each prompt id names exactly 16 candidates. `span_ids`: never falls along the training rows, and every document has at least one row.
All inputs are finite; a program needn't handle non-finite values.
Results may differ from the reference program's by a relative error of at most 0.0042.
Values may be sent and summed in bfloat16 or wider, within the bound.
A program may use at most 64 MiB of HBM per device.

```python
import math
import jax
import jax.numpy as jnp
import numpy as np
from jax import lax

PROJ_IN = 128
PROJ_OUT = 128
K = 16384
CAND_DEV = 160
TRAIN_DEV = 128
DOCS_DEV = 16
NBEST = 16
CANDS = 640
TRAIN = 512
NDOC = 64
GROUPS = 40
N_WIDE = 4


def draw_group_ids(key, part):
    key = jax.random.fold_in(key, 7)
    order = jax.random.permutation(key, CANDS)
    return (order // NBEST).astype(jnp.int32)


def levels(stream_key, shape, pieces, low, high):
    def one(position, shards_of):
        heights = jax.random.uniform(jax.random.fold_in(jax.random.fold_in(stream_key, 6), position), (shards_of,), jnp.float32, low / len(pieces), high / len(pieces))
        return jnp.repeat(jnp.exp(heights), shape[position] // shards_of).reshape((-1,) + (1,) * (len(shape) - position - 1))

    factor_of = one(*pieces[0])
    for cut in pieces[1:]:
        factor_of = factor_of * one(*cut)
    return factor_of


def profile(amount, total, most, skew):
    loads = [(1 << 20) // math.isqrt(standing ** skew) + 1 for standing in range(2, amount + 1)]
    rest, holding = total - most - (amount - 1), [1] * (amount - 1)
    while rest > 0:
        movable = [i for i in range(amount - 1) if holding[i] < most]
        pool, remaining = sum([loads[i] for i in movable]), rest
        for i in movable:
            more = min(most - holding[i], max(1, remaining * loads[i] // pool), rest)
            holding[i] = holding[i] + more
            rest = rest - more
    return np.array([most] + holding)


def ragged(rng, count, total, most, skew):
    if count == 2:
        one = jax.random.randint(rng, (), max(1, total - most), min(most, total - 1) + 1)
        return jnp.stack([one, total - one])
    lengths = jnp.asarray(profile(count, total, most, skew), jnp.int32)
    couples = (count - 1) // 2
    source_of, receiver = lengths[1:1 + 2 * couples:2], lengths[2:2 + 2 * couples:2]
    margin = jnp.minimum(source_of - 1, most - receiver)
    passed = jax.random.randint(jax.random.fold_in(rng, 1), (couples,), 0, 1 << 20) % (margin + 1)
    lengths = lengths.at[1:1 + 2 * couples:2].set(source_of - passed).at[2:2 + 2 * couples:2].set(receiver + passed)
    return lengths[jax.random.permutation(jax.random.fold_in(rng, 2), count)]


def bell_draw(stream_key, shape, spread, most, cuts=(), kind=jnp.bfloat16):
    loudness = levels(stream_key, shape, cuts, -0.22, 0.18) if cuts else 1.0
    array = jax.random.normal(stream_key, shape, jnp.float32) * spread * loudness
    return jnp.minimum(jnp.maximum(array, -most), most).astype(kind)


def setup_inputs(seed: int = 0, part: int = 0) -> dict:
    arg_keys = jax.random.split(jax.random.key(seed), 8)
    part_splits = jax.random.split(jax.random.fold_in(arg_keys[7], part), 8)
    cand_grads = bell_draw(part_splits[0], (CANDS, K), 1.0, 6.0, ((0, 4), (1, 4)))
    train_feats = bell_draw(part_splits[1], (TRAIN, K), K ** -0.5, 0.046875, ((0, 4), (1, 4)))
    span_ids = jnp.searchsorted(jnp.cumsum(ragged(part_splits[2], NDOC, TRAIN, 4 * TRAIN_DEV // DOCS_DEV, 1)), jnp.arange(TRAIN), side="right").astype(jnp.int32)
    group_ids = draw_group_ids(jax.random.fold_in(jax.random.fold_in(arg_keys[7], part), 71), part)
    eig_values = jnp.clip(jnp.exp(jax.random.uniform(arg_keys[4], (PROJ_IN, PROJ_OUT), jnp.float32, math.log(0.05), math.log(2.0))), 0.05, 2.0)
    input_basis = bell_draw(arg_keys[5], (PROJ_IN, PROJ_IN), PROJ_IN ** -0.5, 0.5, (), jnp.float32)
    basis = bell_draw(arg_keys[6], (PROJ_OUT, PROJ_OUT), PROJ_OUT ** -0.5, 0.5, (), jnp.float32)
    return {"cand_grads": cand_grads, "train_feats": train_feats, "span_ids": span_ids, "group_ids": group_ids, "eig_values": eig_values, "input_basis": input_basis, "basis": basis}


damping = 0.05


def precondition(gradients, input_basis, basis, eig_values):
    highest = lax.Precision.HIGHEST
    left_side = jnp.einsum("nab,bc->nac", gradients, basis, precision=highest)
    rotated = jnp.einsum("ae,nac->nec", input_basis, left_side, precision=highest)
    scaled = rotated / (eig_values + damping)
    right_side = jnp.einsum("nec,bc->neb", scaled, basis, precision=highest)
    return jnp.einsum("ae,neb->nab", input_basis, right_side, precision=highest)


def reference(cand_grads, train_feats, span_ids, group_ids, eig_values, input_basis, basis):
    blocks = cand_grads.reshape(N_WIDE, CAND_DEV, PROJ_IN, PROJ_OUT)

    def one_block(block):
        restored = precondition(block.astype(jnp.float32), input_basis, basis, eig_values)
        return restored.reshape(CAND_DEV, K).astype(jnp.bfloat16)

    precond = lax.map(one_block, blocks).reshape(CANDS, K).astype(jnp.float32)
    scores = jnp.dot(precond, train_feats.astype(jnp.float32).T, preferred_element_type=jnp.float32)
    doc_peak = jax.ops.segment_max(scores.T, span_ids, NDOC).T
    group_mean = jax.ops.segment_sum(doc_peak, group_ids, GROUPS) / NBEST
    return doc_peak - group_mean[group_ids]
```

```python
import functools

import jax
import jax.numpy as jnp
from jax import lax
from jax.experimental import pallas as pl
from jax.experimental.pallas import tpu as pltpu
from jax.sharding import PartitionSpec as P

DOCS_DEV = 16
NBEST = 16
SPAN_MOST = 32
CORES = 2
DAMPING = 0.05
LOWEST = -1e30

MESH = pl.DeviceIdType.MESH
HIGHEST = lax.Precision.HIGHEST
ROW_BY_ROW = (((1,), (1,)), ((), ()))


def split(value):
    high = value.astype(jnp.bfloat16)
    return high, (value - high.astype(jnp.float32)).astype(jnp.bfloat16)


def product(left, right):
    return jnp.dot(left, right, preferred_element_type=jnp.float32)


def stack_rows(pieces):
    if pieces[0].shape[0] % 16:
        joined = jnp.concatenate([piece.astype(jnp.float32) for piece in pieces], axis=0)
        return joined.astype(jnp.bfloat16)
    return jnp.concatenate(pieces, axis=0)


def kernel(
    chunks, t_ref, g_ref, span_ref, group_ref, eig_ref, in_ref, basis_ref, out_ref,
    taken, made, held, gathered, scores, shares, peaks_out, peaks_in, sums,
    t_send, t_recv, m_send, m_recv, g_send, g_pass, g_recv, s_send, s_recv,
    p_send, p_recv, q_send, q_recv, t_local, g_local,
):
    wide, narrow = lax.axis_size("wide"), lax.axis_size("narrow")
    w, z = lax.axis_index("wide"), lax.axis_index("narrow")
    chips = wide // CORES
    chip, core = w // CORES, lax.rem(w, CORES)
    sibling = chip * CORES + 1 - core
    rows = taken.shape[2]
    local_in = taken.shape[3] // 128
    size = basis_ref.shape[0]

    def other(index, step, count):
        return lax.rem(index + step, count)

    def remote(source, target, send, recv, device):
        return pltpu.make_async_remote_copy(
            src_ref=source, dst_ref=target, send_sem=send, recv_sem=recv,
            device_id=device, device_id_type=MESH,
        )

    def rows_copy(chunk, peer, slot):
        return remote(
            t_ref.at[chunk, peer], taken.at[chunk, slot],
            t_send.at[chunk, peer], t_recv.at[chunk, slot], {"narrow": peer},
        )

    def made_copy(chunk, peer, slot):
        return remote(
            made.at[chunk, peer], held.at[chunk, slot],
            m_send.at[chunk, peer], m_recv.at[chunk, slot], {"narrow": peer},
        )

    def grad_copy(there, slot):
        return remote(
            g_ref, gathered.at[slot], g_send.at[there], g_recv.at[slot],
            {"wide": there * CORES + core},
        )

    def pass_copy(here, slot):
        return remote(
            gathered.at[slot], gathered.at[slot], g_pass.at[here], g_recv.at[slot], {"wide": sibling}
        )

    def own_pass(slot):
        return remote(g_ref, gathered.at[slot], g_pass.at[chip], g_recv.at[slot], {"wide": sibling})

    def share_copy(peer, slot):
        return remote(
            scores.at[peer], shares.at[slot], s_send.at[peer], s_recv.at[slot], {"narrow": peer}
        )

    def peak_copy(docs, slot):
        return remote(
            peaks_out.at[docs], peaks_in.at[slot], p_send.at[docs], p_recv.at[slot],
            {"wide": z, "narrow": docs},
        )

    def sum_copy(peer, slot):
        return remote(sums.at[w], sums.at[slot], q_send.at[peer], q_recv.at[slot], {"wide": peer})

    barrier = pltpu.get_barrier_semaphore()
    for step in range(1, narrow):
        pl.semaphore_signal(
            barrier, inc=1, device_id={"narrow": other(z, step, narrow)}, device_id_type=MESH
        )
    for step in range(1, wide):
        peer = other(w, step, wide)
        pl.semaphore_signal(barrier, inc=1, device_id={"wide": peer}, device_id_type=MESH)
        pl.semaphore_signal(
            barrier, inc=1, device_id={"wide": peer, "narrow": w}, device_id_type=MESH
        )
    pl.semaphore_wait(barrier, narrow - 1 + wide - 1 + jnp.where(w == z, 0, narrow))

    own_rows = [
        pltpu.make_async_copy(t_ref.at[chunk, z], taken.at[chunk, z], t_local.at[chunk])
        for chunk in range(chunks)
    ]
    own_grads = pltpu.make_async_copy(g_ref, gathered.at[w], g_local)
    for chunk in range(chunks):
        for step in range(1, narrow):
            rows_copy(chunk, other(z, step, narrow), z).start()
        own_rows[chunk].start()
        if chunk == 0:
            for step in range(1, chips):
                grad_copy(other(chip, step, chips), w).start()
            own_pass(w).start()
            own_grads.start()

    in_basis, out_basis = in_ref[...], basis_ref[...]
    in_high, in_low = split(in_basis)
    inT_high, inT_low = split(in_basis.T)
    out_high, out_low = split(out_basis)
    outT_high, outT_low = split(out_basis.T)
    into = jnp.concatenate([out_high, out_low], axis=1)
    back = jnp.concatenate(
        [
            jnp.concatenate([outT_high, outT_low], axis=1),
            jnp.concatenate([outT_high, jnp.zeros_like(outT_low)], axis=1),
        ],
        axis=0,
    )
    in_into = jnp.concatenate([inT_high, inT_high, inT_low], axis=1)
    in_back = jnp.concatenate([in_high, in_high, in_low], axis=1)
    weight = 1.0 / (eig_ref[...] + DAMPING)

    def mixed(matrix, blocks):
        wide_block = jnp.concatenate(blocks, axis=1)
        high, low = split(wide_block)
        return product(matrix, jnp.concatenate([high, low, high], axis=0))

    def lane_block(value, index):
        return value[:, index * size : (index + 1) * size]

    def precondition(chunk):
        pieces = [
            taken[chunk, source, :, a * size : (a + 1) * size]
            for source in range(narrow)
            for a in range(local_in)
        ]
        both = product(stack_rows(pieces), into)
        left = both[:, :size] + both[:, size:]
        left = jnp.swapaxes(left.reshape(size, rows, size), 0, 1)
        rotated = mixed(in_into, [left[row] for row in range(rows)])
        scaled = jnp.concatenate([lane_block(rotated, row) * weight for row in range(rows)], axis=0)
        both = product(jnp.concatenate(split(scaled), axis=1), back)
        right = both[:, :size] + both[:, size:]
        restored = mixed(in_back, [right[row * size : (row + 1) * size] for row in range(rows)])
        result = jnp.stack([lane_block(restored, row) for row in range(rows)], axis=0)
        result = jnp.swapaxes(result, 0, 1).astype(jnp.bfloat16)
        for target in range(narrow):
            for a in range(local_in):
                made[chunk, target, :, a * size : (a + 1) * size] = result[target * local_in + a]

    for chunk in range(chunks):
        own_rows[chunk].wait()
        for step in range(1, narrow):
            rows_copy(chunk, z, other(z, step, narrow)).wait_recv()
        precondition(chunk)
        for step in range(1, narrow):
            made_copy(chunk, other(z, step, narrow), z).start()
        held[chunk, z] = made[chunk, z]

    for step in range(1, chips):
        there = other(chip, step, chips)
        slot = there * CORES + core
        grad_copy(there, slot).wait_recv()
        pass_copy(there, slot).start()
    own_grads.wait()
    for step in range(chips):
        there = other(chip, step, chips)
        pass_copy(there, there * CORES + 1 - core).wait_recv()

    for chunk in range(chunks):
        for step in range(1, narrow):
            made_copy(chunk, z, other(z, step, narrow)).wait_recv()
        width = narrow * rows

        def score(block, unused, chunk=chunk, width=width):
            train = stack_rows([held[chunk, source] for source in range(narrow)])
            scores[block, :, chunk * width : (chunk + 1) * width] = lax.dot_general(
                gathered[block], train, ROW_BY_ROW, preferred_element_type=jnp.float32
            )
            return unused

        lax.fori_loop(0, wide, score, 0)

    for step in range(1, narrow):
        share_copy(other(z, step, narrow), z).start()
    span = jnp.broadcast_to(span_ref[pl.ds(w, 1), :], (8, span_ref.shape[1]))
    lane = lax.broadcasted_iota(jnp.int32, span.shape, 1)
    row_count = span.shape[1]
    total = scores[z]
    for step in range(1, narrow):
        source = other(z, step, narrow)
        share_copy(z, source).wait_recv()
        total = total + shares[source]

    distance = 1
    while distance < min(SPAN_MOST, row_count):
        same = (pltpu.roll(span, distance, 1) == span) & (lane >= distance)
        earlier = jnp.where(same[:1], pltpu.roll(total, distance, 1), total)
        total = jnp.maximum(total, earlier)
        distance *= 2
    last = (pltpu.roll(span, row_count - 1, 1) != span) | (lane == row_count - 1)
    doc_share = peaks_out.shape[1]
    docs = doc_share * narrow
    wanted = lax.broadcasted_iota(jnp.int32, (docs, row_count), 0)
    pick = ((span[:1] == wanted) & last[:1]).astype(jnp.float32)
    peaks = lax.dot_general(
        pick, total, ROW_BY_ROW, precision=HIGHEST, preferred_element_type=jnp.float32
    )
    peaks = jnp.where(jnp.sum(pick, axis=1, keepdims=True) > 0, peaks, LOWEST)
    for index in range(narrow):
        peaks_out[index] = peaks[index * doc_share : (index + 1) * doc_share]
    for step in range(1, narrow):
        peak_copy(other(z, step, narrow), w).start()

    @pl.when(w != z)
    def _():
        peak_copy(z, w).start()

    @pl.when(w == z)
    def _():
        peaks_in[w] = peaks_out[z]

    group_slots = sums.shape[2]
    cands = group_ref.shape[1]
    member = (
        group_ref[...] == lax.broadcasted_iota(jnp.int32, (group_slots, cands), 0)
    ).astype(jnp.float32)
    for step in range(1, wide):
        peak_copy(z, other(w, step, wide)).wait_recv()

    @pl.when(w != z)
    def _():
        peak_copy(z, w).wait_recv()

    doc_peak = peaks_in[0]
    for index in range(1, wide):
        doc_peak = jnp.maximum(doc_peak, peaks_in[index])
    sums[w] = lax.dot_general(
        doc_peak, member, ROW_BY_ROW, precision=HIGHEST, preferred_element_type=jnp.float32
    )
    for step in range(1, wide):
        sum_copy(other(w, step, wide), w).start()
    for step in range(1, wide):
        sum_copy(w, other(w, step, wide)).wait_recv()
    mean = sums[0]
    for index in range(1, wide):
        mean = mean + sums[index]
    out_ref[...] = doc_peak - jnp.dot(
        mean * (1.0 / NBEST), member, precision=HIGHEST, preferred_element_type=jnp.float32
    )

    for chunk in range(chunks):
        for step in range(1, narrow):
            rows_copy(chunk, other(z, step, narrow), z).wait_send()
            made_copy(chunk, other(z, step, narrow), z).wait_send()
    for step in range(1, chips):
        there = other(chip, step, chips)
        grad_copy(there, w).wait_send()
        pass_copy(there, there * CORES + core).wait_send()
    own_pass(w).wait_send()
    for step in range(1, narrow):
        share_copy(other(z, step, narrow), z).wait_send()
        peak_copy(other(z, step, narrow), w).wait_send()

    @pl.when(w != z)
    def _():
        peak_copy(z, w).wait_send()

    for step in range(1, wide):
        sum_copy(other(w, step, wide), w).wait_send()


def solution(mesh):
    wide, narrow = mesh.shape["wide"], mesh.shape["narrow"]
    assert wide == narrow

    def local(cand_grads, train_feats, span_ids, group_ids, eig_values, input_basis, basis):
        cands, width = cand_grads.shape
        train_rows = train_feats.shape[0]
        peer_rows = train_rows // narrow
        chunks = max(1, peer_rows // 16)
        rows = peer_rows // chunks
        doc_share = DOCS_DEV * wide // narrow
        group_slots = -(-(cands * wide // NBEST) // 128) * 128
        in_vmem = pl.BlockSpec(memory_space=pltpu.VMEM)
        anywhere = pl.BlockSpec(memory_space=pl.ANY)
        dma = pltpu.SemaphoreType.DMA
        turned = pl.pallas_call(
            functools.partial(kernel, chunks),
            out_shape=jax.ShapeDtypeStruct((doc_share, cands), jnp.float32),
            in_specs=[anywhere, anywhere] + [in_vmem] * 5,
            out_specs=in_vmem,
            scratch_shapes=[
                pltpu.VMEM((chunks, narrow, rows, width), jnp.bfloat16),
                pltpu.VMEM((chunks, narrow, rows, width), jnp.bfloat16),
                pltpu.VMEM((chunks, narrow, rows, width), jnp.bfloat16),
                pltpu.VMEM((wide, cands, width), jnp.bfloat16),
                pltpu.VMEM((wide, cands, train_rows), jnp.float32),
                pltpu.VMEM((narrow, cands, train_rows), jnp.float32),
                pltpu.VMEM((narrow, doc_share, cands), jnp.float32),
                pltpu.VMEM((wide, doc_share, cands), jnp.float32),
                pltpu.VMEM((wide, doc_share, group_slots), jnp.float32),
                dma((chunks, narrow)),
                dma((chunks, narrow)),
                dma((chunks, narrow)),
                dma((chunks, narrow)),
                dma((wide // CORES,)),
                dma((wide // CORES,)),
                dma((wide,)),
                dma((narrow,)),
                dma((narrow,)),
                dma((narrow,)),
                dma((wide,)),
                dma((wide,)),
                dma((wide,)),
                dma((chunks,)),
                dma(()),
            ],
            compiler_params=pltpu.CompilerParams(
                collective_id=0, has_side_effects=True, vmem_limit_bytes=48 * 2**20
            ),
        )(
            train_feats.reshape(chunks, narrow, rows, width),
            cand_grads,
            span_ids.reshape(wide, train_rows),
            group_ids.reshape(1, cands),
            eig_values,
            input_basis,
            basis,
        )
        return turned.T

    return jax.shard_map(
        local,
        mesh=mesh,
        in_specs=(
            P(("parts", "wide"), "narrow"),
            P(("parts", "wide"), "narrow"),
            P("parts"),
            P(("parts", "wide")),
            P(),
            P(),
            P(),
        ),
        out_specs=P(("parts", "wide"), "narrow"),
        check_vma=False,
    )
```

```python
import functools

import jax
import jax.numpy as jnp
from jax import lax
from jax.experimental import pallas as pl
from jax.experimental.pallas import tpu as pltpu
from jax.sharding import PartitionSpec as P

DOCS_DEV = 16
NBEST = 16
SPAN_MOST = 32
CORES = 2
DAMPING = 0.05
LOWEST = -1e30

MESH = pl.DeviceIdType.MESH
HIGHEST = lax.Precision.HIGHEST
ROW_BY_ROW = (((1,), (1,)), ((), ()))


def split(value):
    high = value.astype(jnp.bfloat16)
    return high, (value - high.astype(jnp.float32)).astype(jnp.bfloat16)


def product(left, right):
    return jnp.dot(left, right, preferred_element_type=jnp.float32)


def stack_rows(pieces):
    if pieces[0].shape[0] % 16:
        joined = jnp.concatenate([piece.astype(jnp.float32) for piece in pieces], axis=0)
        return joined.astype(jnp.bfloat16)
    return jnp.concatenate(pieces, axis=0)


def kernel(
    chunks, t_ref, g_ref, span_hbm, group_hbm, eig_hbm, in_hbm, basis_hbm, out_ref,
    span_ref, group_ref, eig_ref, in_ref, basis_ref, taken, made, held, gathered, scores, shares, peaks_out, peaks_in, sums,
    t_send, t_recv, m_send, m_recv, g_send, g_pass, g_recv, s_send, s_recv,
    p_send, p_recv, q_send, q_recv, t_local, g_local, small,
):
    wide, narrow = lax.axis_size("wide"), lax.axis_size("narrow")
    w, z = lax.axis_index("wide"), lax.axis_index("narrow")
    chips = wide // CORES
    chip, core = w // CORES, lax.rem(w, CORES)
    sibling = chip * CORES + 1 - core
    rows = taken.shape[2]
    local_in = taken.shape[3] // 128
    size = basis_ref.shape[0]

    def other(index, step, count):
        return lax.rem(index + step, count)

    def remote(source, target, send, recv, device):
        return pltpu.make_async_remote_copy(
            src_ref=source, dst_ref=target, send_sem=send, recv_sem=recv,
            device_id=device, device_id_type=MESH,
        )

    def rows_copy(chunk, peer, slot):
        return remote(
            t_ref.at[chunk, peer], taken.at[chunk, slot],
            t_send.at[chunk, peer], t_recv.at[chunk, slot], {"narrow": peer},
        )

    def made_copy(chunk, peer, slot):
        return remote(
            made.at[chunk, peer], held.at[chunk, slot],
            m_send.at[chunk, peer], m_recv.at[chunk, slot], {"narrow": peer},
        )

    def grad_copy(there, slot):
        return remote(
            g_ref, gathered.at[slot], g_send.at[there], g_recv.at[slot],
            {"wide": there * CORES + core},
        )

    def pass_copy(here, slot):
        return remote(
            gathered.at[slot], gathered.at[slot], g_pass.at[here], g_recv.at[slot], {"wide": sibling}
        )

    def own_pass(slot):
        return remote(g_ref, gathered.at[slot], g_pass.at[chip], g_recv.at[slot], {"wide": sibling})

    def share_copy(peer, slot):
        return remote(
            scores.at[peer], shares.at[slot], s_send.at[peer], s_recv.at[slot], {"narrow": peer}
        )

    def peak_copy(docs, slot):
        return remote(
            peaks_out.at[docs], peaks_in.at[slot], p_send.at[docs], p_recv.at[slot],
            {"wide": z, "narrow": docs},
        )

    def sum_copy(peer, slot):
        return remote(sums.at[w], sums.at[slot], q_send.at[peer], q_recv.at[slot], {"wide": peer})

    fetches = [
        pltpu.make_async_copy(source, target, small.at[index])
        for index, (source, target) in enumerate(
            (
                (in_hbm, in_ref),
                (basis_hbm, basis_ref),
                (eig_hbm, eig_ref),
                (span_hbm, span_ref),
                (group_hbm, group_ref),
            )
        )
    ]
    for fetch in fetches:
        fetch.start()
    barrier = pltpu.get_barrier_semaphore()
    for step in range(1, narrow):
        pl.semaphore_signal(
            barrier, inc=1, device_id={"narrow": other(z, step, narrow)}, device_id_type=MESH
        )
    for step in range(1, wide):
        peer = other(w, step, wide)
        pl.semaphore_signal(barrier, inc=1, device_id={"wide": peer}, device_id_type=MESH)
        pl.semaphore_signal(
            barrier, inc=1, device_id={"wide": peer, "narrow": w}, device_id_type=MESH
        )
    pl.semaphore_wait(barrier, narrow - 1 + wide - 1 + jnp.where(w == z, 0, narrow))

    own_rows = [
        pltpu.make_async_copy(t_ref.at[chunk, z], taken.at[chunk, z], t_local.at[chunk])
        for chunk in range(chunks)
    ]
    own_grads = pltpu.make_async_copy(g_ref, gathered.at[w], g_local)
    for chunk in range(chunks):
        for step in range(1, narrow):
            rows_copy(chunk, other(z, step, narrow), z).start()
        own_rows[chunk].start()
        if chunk == 0:
            for step in range(1, chips):
                grad_copy(other(chip, step, chips), w).start()
            own_pass(w).start()
            own_grads.start()

    for fetch in fetches:
        fetch.wait()
    in_basis, out_basis = in_ref[...], basis_ref[...]
    in_high, in_low = split(in_basis)
    inT_high, inT_low = split(in_basis.T)
    out_high, out_low = split(out_basis)
    outT_high, outT_low = split(out_basis.T)
    into = jnp.concatenate([out_high, out_low], axis=1)
    back = jnp.concatenate(
        [
            jnp.concatenate([outT_high, outT_low], axis=1),
            jnp.concatenate([outT_high, jnp.zeros_like(outT_low)], axis=1),
        ],
        axis=0,
    )
    in_into = jnp.concatenate([inT_high, inT_high, inT_low], axis=1)
    in_back = jnp.concatenate([in_high, in_high, in_low], axis=1)
    weight = 1.0 / (eig_ref[...] + DAMPING)

    def mixed(matrix, blocks):
        wide_block = jnp.concatenate(blocks, axis=1)
        high, low = split(wide_block)
        return product(matrix, jnp.concatenate([high, low, high], axis=0))

    def lane_block(value, index):
        return value[:, index * size : (index + 1) * size]

    def precondition(chunk):
        pieces = [
            taken[chunk, source, :, a * size : (a + 1) * size]
            for source in range(narrow)
            for a in range(local_in)
        ]
        both = product(stack_rows(pieces), into)
        left = both[:, :size] + both[:, size:]
        left = jnp.swapaxes(left.reshape(size, rows, size), 0, 1)
        rotated = mixed(in_into, [left[row] for row in range(rows)])
        scaled = jnp.concatenate([lane_block(rotated, row) * weight for row in range(rows)], axis=0)
        both = product(jnp.concatenate(split(scaled), axis=1), back)
        right = both[:, :size] + both[:, size:]
        restored = mixed(in_back, [right[row * size : (row + 1) * size] for row in range(rows)])
        result = jnp.stack([lane_block(restored, row) for row in range(rows)], axis=0)
        result = jnp.swapaxes(result, 0, 1).astype(jnp.bfloat16)
        for target in range(narrow):
            for a in range(local_in):
                made[chunk, target, :, a * size : (a + 1) * size] = result[target * local_in + a]

    for chunk in range(chunks):
        own_rows[chunk].wait()
        for step in range(1, narrow):
            rows_copy(chunk, z, other(z, step, narrow)).wait_recv()
        precondition(chunk)
        for step in range(1, narrow):
            made_copy(chunk, other(z, step, narrow), z).start()
        held[chunk, z] = made[chunk, z]

    for step in range(1, chips):
        there = other(chip, step, chips)
        slot = there * CORES + core
        grad_copy(there, slot).wait_recv()
        pass_copy(there, slot).start()
    own_grads.wait()
    for step in range(chips):
        there = other(chip, step, chips)
        pass_copy(there, there * CORES + 1 - core).wait_recv()

    for chunk in range(chunks):
        for step in range(1, narrow):
            made_copy(chunk, z, other(z, step, narrow)).wait_recv()
        width = narrow * rows

        def score(block, unused, chunk=chunk, width=width):
            train = stack_rows([held[chunk, source] for source in range(narrow)])
            scores[block, :, chunk * width : (chunk + 1) * width] = lax.dot_general(
                gathered[block], train, ROW_BY_ROW, preferred_element_type=jnp.float32
            )
            return unused

        lax.fori_loop(0, wide, score, 0)

    for step in range(1, narrow):
        share_copy(other(z, step, narrow), z).start()
    span = jnp.broadcast_to(span_ref[pl.ds(w, 1), :], (8, span_ref.shape[1]))
    lane = lax.broadcasted_iota(jnp.int32, span.shape, 1)
    row_count = span.shape[1]
    total = scores[z]
    for step in range(1, narrow):
        source = other(z, step, narrow)
        share_copy(z, source).wait_recv()
        total = total + shares[source]

    distance = 1
    while distance < min(SPAN_MOST, row_count):
        same = (pltpu.roll(span, distance, 1) == span) & (lane >= distance)
        earlier = jnp.where(same[:1], pltpu.roll(total, distance, 1), total)
        total = jnp.maximum(total, earlier)
        distance *= 2
    last = (pltpu.roll(span, row_count - 1, 1) != span) | (lane == row_count - 1)
    doc_share = peaks_out.shape[1]
    docs = doc_share * narrow
    wanted = lax.broadcasted_iota(jnp.int32, (docs, row_count), 0)
    pick = ((span[:1] == wanted) & last[:1]).astype(jnp.float32)
    peaks = lax.dot_general(
        pick, total, ROW_BY_ROW, precision=HIGHEST, preferred_element_type=jnp.float32
    )
    peaks = jnp.where(jnp.sum(pick, axis=1, keepdims=True) > 0, peaks, LOWEST)
    for index in range(narrow):
        peaks_out[index] = peaks[index * doc_share : (index + 1) * doc_share]
    for step in range(1, narrow):
        peak_copy(other(z, step, narrow), w).start()

    @pl.when(w != z)
    def _():
        peak_copy(z, w).start()

    @pl.when(w == z)
    def _():
        peaks_in[w] = peaks_out[z]

    group_slots = sums.shape[2]
    cands = group_ref.shape[1]
    member = (
        group_ref[...] == lax.broadcasted_iota(jnp.int32, (group_slots, cands), 0)
    ).astype(jnp.float32)
    for step in range(1, wide):
        peak_copy(z, other(w, step, wide)).wait_recv()

    @pl.when(w != z)
    def _():
        peak_copy(z, w).wait_recv()

    doc_peak = peaks_in[0]
    for index in range(1, wide):
        doc_peak = jnp.maximum(doc_peak, peaks_in[index])
    sums[w] = lax.dot_general(
        doc_peak, member, ROW_BY_ROW, precision=HIGHEST, preferred_element_type=jnp.float32
    )
    for step in range(1, wide):
        sum_copy(other(w, step, wide), w).start()
    for step in range(1, wide):
        sum_copy(w, other(w, step, wide)).wait_recv()
    mean = sums[0]
    for index in range(1, wide):
        mean = mean + sums[index]
    out_ref[...] = doc_peak - jnp.dot(
        mean * (1.0 / NBEST), member, precision=HIGHEST, preferred_element_type=jnp.float32
    )

    for chunk in range(chunks):
        for step in range(1, narrow):
            rows_copy(chunk, other(z, step, narrow), z).wait_send()
            made_copy(chunk, other(z, step, narrow), z).wait_send()
    for step in range(1, chips):
        there = other(chip, step, chips)
        grad_copy(there, w).wait_send()
        pass_copy(there, there * CORES + core).wait_send()
    own_pass(w).wait_send()
    for step in range(1, narrow):
        share_copy(other(z, step, narrow), z).wait_send()
        peak_copy(other(z, step, narrow), w).wait_send()

    @pl.when(w != z)
    def _():
        peak_copy(z, w).wait_send()

    for step in range(1, wide):
        sum_copy(other(w, step, wide), w).wait_send()


def solution(mesh):
    wide, narrow = mesh.shape["wide"], mesh.shape["narrow"]
    assert wide == narrow

    def local(cand_grads, train_feats, span_ids, group_ids, eig_values, input_basis, basis):
        cands, width = cand_grads.shape
        train_rows = train_feats.shape[0]
        peer_rows = train_rows // narrow
        chunks = max(1, peer_rows // 16)
        rows = peer_rows // chunks
        doc_share = DOCS_DEV * wide // narrow
        group_slots = -(-(cands * wide // NBEST) // 128) * 128
        in_vmem = pl.BlockSpec(memory_space=pltpu.VMEM)
        anywhere = pl.BlockSpec(memory_space=pltpu.HBM)
        dma = pltpu.SemaphoreType.DMA
        turned = pl.pallas_call(
            functools.partial(kernel, chunks),
            out_shape=jax.ShapeDtypeStruct((doc_share, cands), jnp.float32),
            in_specs=[anywhere] * 7,
            out_specs=in_vmem,
            scratch_shapes=[
                pltpu.VMEM((wide, train_rows), jnp.int32),
                pltpu.VMEM((1, cands), jnp.int32),
                pltpu.VMEM(eig_values.shape, jnp.float32),
                pltpu.VMEM(input_basis.shape, jnp.float32),
                pltpu.VMEM(basis.shape, jnp.float32),
                pltpu.VMEM((chunks, narrow, rows, width), jnp.bfloat16),
                pltpu.VMEM((chunks, narrow, rows, width), jnp.bfloat16),
                pltpu.VMEM((chunks, narrow, rows, width), jnp.bfloat16),
                pltpu.VMEM((wide, cands, width), jnp.bfloat16),
                pltpu.VMEM((wide, cands, train_rows), jnp.float32),
                pltpu.VMEM((narrow, cands, train_rows), jnp.float32),
                pltpu.VMEM((narrow, doc_share, cands), jnp.float32),
                pltpu.VMEM((wide, doc_share, cands), jnp.float32),
                pltpu.VMEM((wide, doc_share, group_slots), jnp.float32),
                dma((chunks, narrow)),
                dma((chunks, narrow)),
                dma((chunks, narrow)),
                dma((chunks, narrow)),
                dma((wide // CORES,)),
                dma((wide // CORES,)),
                dma((wide,)),
                dma((narrow,)),
                dma((narrow,)),
                dma((narrow,)),
                dma((wide,)),
                dma((wide,)),
                dma((wide,)),
                dma((chunks,)),
                dma(()),
                dma((5,)),
            ],
            compiler_params=pltpu.CompilerParams(
                collective_id=0, has_side_effects=True, vmem_limit_bytes=63 * 2**20
            ),
        )(
            train_feats.reshape(chunks, narrow, rows, width),
            cand_grads,
            span_ids.reshape(wide, train_rows),
            group_ids.reshape(1, cands),
            eig_values,
            input_basis,
            basis,
        )
        return turned.T

    return jax.shard_map(
        local,
        mesh=mesh,
        in_specs=(
            P(("parts", "wide"), "narrow"),
            P(("parts", "wide"), "narrow"),
            P("parts"),
            P(("parts", "wide")),
            P(),
            P(),
            P(),
        ),
        out_specs=P(("parts", "wide"), "narrow"),
        check_vma=False,
    )
```

```python
import functools

import jax
import jax.numpy as jnp
from jax import lax
from jax.experimental import pallas as pl
from jax.experimental.pallas import tpu as pltpu
from jax.sharding import PartitionSpec as P

DOCS_DEV = 16
NBEST = 16
SPAN_MOST = 32
CORES = 2
DAMPING = 0.05
LOWEST = -1e30

MESH = pl.DeviceIdType.MESH
HIGHEST = lax.Precision.HIGHEST
ROW_BY_ROW = (((1,), (1,)), ((), ()))


def split(value):
    high = value.astype(jnp.bfloat16)
    return high, (value - high.astype(jnp.float32)).astype(jnp.bfloat16)


def product(left, right):
    return jnp.dot(left, right, preferred_element_type=jnp.float32)


def stack_rows(pieces):
    if pieces[0].shape[0] % 16:
        joined = jnp.concatenate([piece.astype(jnp.float32) for piece in pieces], axis=0)
        return joined.astype(jnp.bfloat16)
    return jnp.concatenate(pieces, axis=0)


def kernel(
    chunks, t_ref, g_ref, span_hbm, group_hbm, eig_hbm, in_hbm, basis_hbm, out_ref,
    span_ref, group_ref, eig_ref, in_ref, basis_ref, taken, made, held, gathered, scores, shares, low, coarse, coarse_in, peaks_out, peaks_in, sums,
    t_send, t_recv, m_send, m_recv, g_send, g_pass, g_recv, s_send, s_recv, c_send, c_recv,
    p_send, p_recv, q_send, q_recv, t_local, g_local, small,
):
    wide, narrow = lax.axis_size("wide"), lax.axis_size("narrow")
    w, z = lax.axis_index("wide"), lax.axis_index("narrow")
    chips = wide // CORES
    chip, core = w // CORES, lax.rem(w, CORES)
    sibling = chip * CORES + 1 - core
    rows = taken.shape[2]
    local_in = taken.shape[3] // 128
    size = basis_ref.shape[0]
    pieces_out = m_send.shape[1]
    piece_width = taken.shape[3] // pieces_out

    def other(index, step, count):
        return lax.rem(index + step, count)

    def remote(source, target, send, recv, device):
        return pltpu.make_async_remote_copy(
            src_ref=source, dst_ref=target, send_sem=send, recv_sem=recv,
            device_id=device, device_id_type=MESH,
        )

    def rows_copy(chunk, peer, slot):
        return remote(
            t_ref.at[chunk, peer], taken.at[chunk, slot],
            t_send.at[chunk, peer], t_recv.at[chunk, slot], {"narrow": peer},
        )

    def made_copy(chunk, piece, peer, slot):
        columns = pl.ds(piece * piece_width, piece_width)
        return remote(
            made.at[chunk, peer, :, columns], held.at[chunk, slot, :, columns],
            m_send.at[chunk, piece, peer], m_recv.at[chunk, piece, slot], {"narrow": peer},
        )

    def grad_copy(there, slot):
        return remote(
            g_ref, gathered.at[slot], g_send.at[there], g_recv.at[slot],
            {"wide": there * CORES + core},
        )

    def pass_copy(here, slot):
        return remote(
            gathered.at[slot], gathered.at[slot], g_pass.at[here], g_recv.at[slot], {"wide": sibling}
        )

    def own_pass(slot):
        return remote(g_ref, gathered.at[slot], g_pass.at[chip], g_recv.at[slot], {"wide": sibling})

    def share_copy(peer, slot):
        return remote(
            scores.at[peer], shares.at[slot], s_send.at[peer], s_recv.at[slot], {"narrow": peer}
        )

    half = narrow // 2
    near_base = z // half * half
    far_base = half - near_base

    def near(step):
        return near_base + lax.rem(z + step, half)

    def far(step):
        return far_base + lax.rem(z + step, half)

    def coarse_copy(step, slot):
        return remote(
            coarse.at[step], coarse_in.at[slot], c_send.at[step], c_recv.at[slot],
            {"narrow": far(step)},
        )

    def peak_copy(docs, slot):
        return remote(
            peaks_out.at[docs], peaks_in.at[slot], p_send.at[docs], p_recv.at[slot],
            {"wide": z, "narrow": docs},
        )

    def sum_copy(peer, slot):
        return remote(sums.at[w], sums.at[slot], q_send.at[peer], q_recv.at[slot], {"wide": peer})

    fetches = [
        pltpu.make_async_copy(source, target, small.at[index])
        for index, (source, target) in enumerate(
            (
                (in_hbm, in_ref),
                (basis_hbm, basis_ref),
                (eig_hbm, eig_ref),
                (span_hbm, span_ref),
                (group_hbm, group_ref),
            )
        )
    ]
    for fetch in fetches:
        fetch.start()
    barrier = pltpu.get_barrier_semaphore()
    for step in range(1, narrow):
        pl.semaphore_signal(
            barrier, inc=1, device_id={"narrow": other(z, step, narrow)}, device_id_type=MESH
        )
    for step in range(1, wide):
        peer = other(w, step, wide)
        pl.semaphore_signal(barrier, inc=1, device_id={"wide": peer}, device_id_type=MESH)
        pl.semaphore_signal(
            barrier, inc=1, device_id={"wide": peer, "narrow": w}, device_id_type=MESH
        )
    pl.semaphore_wait(barrier, narrow - 1 + wide - 1 + jnp.where(w == z, 0, narrow))

    own_rows = [
        pltpu.make_async_copy(t_ref.at[chunk, z], taken.at[chunk, z], t_local.at[chunk])
        for chunk in range(chunks)
    ]
    own_grads = pltpu.make_async_copy(g_ref, gathered.at[w], g_local)
    for chunk in range(chunks):
        for step in range(1, narrow):
            rows_copy(chunk, other(z, step, narrow), z).start()
        own_rows[chunk].start()
        if chunk == 0:
            for step in range(1, chips):
                grad_copy(other(chip, step, chips), w).start()
            own_pass(w).start()
            own_grads.start()

    for fetch in fetches:
        fetch.wait()
    in_basis, out_basis = in_ref[...], basis_ref[...]
    in_high, in_low = split(in_basis)
    inT_high, inT_low = split(in_basis.T)
    out_high, out_low = split(out_basis)
    outT_high, outT_low = split(out_basis.T)
    into = jnp.concatenate([out_high, out_low], axis=1)
    back = jnp.concatenate(
        [
            jnp.concatenate([outT_high, outT_low], axis=1),
            jnp.concatenate([outT_high, jnp.zeros_like(outT_low)], axis=1),
        ],
        axis=0,
    )
    in_into = jnp.concatenate([inT_high, inT_high, inT_low], axis=1)
    in_back = jnp.concatenate([in_high, in_high, in_low], axis=1)
    weight = 1.0 / (eig_ref[...] + DAMPING)

    def mixed(matrix, blocks):
        wide_block = jnp.concatenate(blocks, axis=1)
        high, low = split(wide_block)
        return product(matrix, jnp.concatenate([high, low, high], axis=0))

    def lane_block(value, index):
        return value[:, index * size : (index + 1) * size]

    def precondition(chunk):
        pieces = [
            taken[chunk, source, :, a * size : (a + 1) * size]
            for source in range(narrow)
            for a in range(local_in)
        ]
        both = product(stack_rows(pieces), into)
        left = both[:, :size] + both[:, size:]
        left = jnp.swapaxes(left.reshape(size, rows, size), 0, 1)
        rotated = mixed(in_into, [left[row] for row in range(rows)])
        scaled = jnp.concatenate([lane_block(rotated, row) * weight for row in range(rows)], axis=0)
        both = product(jnp.concatenate(split(scaled), axis=1), back)
        right = both[:, :size] + both[:, size:]
        restored = mixed(in_back, [right[row * size : (row + 1) * size] for row in range(rows)])
        result = jnp.stack([lane_block(restored, row) for row in range(rows)], axis=0)
        exact = jnp.swapaxes(result, 0, 1)
        result = exact.astype(jnp.bfloat16)
        rest = exact - result.astype(jnp.float32)
        for target in range(narrow):
            for a in range(local_in):
                made[chunk, target, :, a * size : (a + 1) * size] = result[target * local_in + a]
            keep = jnp.where(z == target, 1.0, 0.0)
            for a in range(local_in):
                low[chunk, target, :, a * size : (a + 1) * size] = (
                    rest[target * local_in + a] * keep
                ).astype(jnp.bfloat16)

    for chunk in range(chunks):
        own_rows[chunk].wait()
        for step in range(1, narrow):
            rows_copy(chunk, z, other(z, step, narrow)).wait_recv()
        precondition(chunk)
        for piece in range(pieces_out):
            for step in range(1, narrow):
                made_copy(chunk, piece, other(z, step, narrow), z).start()
        held[chunk, z] = made[chunk, z]

    for step in range(1, chips):
        there = other(chip, step, chips)
        slot = there * CORES + core
        grad_copy(there, slot).wait_recv()
        pass_copy(there, slot).start()
    own_grads.wait()
    for step in range(chips):
        there = other(chip, step, chips)
        pass_copy(there, there * CORES + 1 - core).wait_recv()

    def score(chunk, piece, block):
        width = narrow * rows
        place = (block, slice(None), slice(chunk * width, (chunk + 1) * width))
        columns = slice(piece * piece_width, (piece + 1) * piece_width)
        train = stack_rows(
            [part[chunk, source, :, columns] for part in (held, low) for source in range(narrow)]
        )
        value = lax.dot_general(
            gathered[block, :, columns], train, ROW_BY_ROW, preferred_element_type=jnp.float32
        )
        value = value[:, :width] + value[:, width:]
        scores[place] = value if piece == 0 else scores[place] + value

    for chunk in range(chunks):
        for piece in range(pieces_out):
            for step in range(1, narrow):
                made_copy(chunk, piece, z, other(z, step, narrow)).wait_recv()
            if chunk == chunks - 1 and piece == pieces_out - 1:
                for step in range(half):
                    block = far(step)
                    score(chunk, piece, block)
                    coarse[step] = scores[block].astype(jnp.bfloat16)
                    coarse_copy(step, lax.rem(z, half)).start()
                for step in range(1, half):
                    block = near(step)
                    score(chunk, piece, block)
                    share_copy(block, z).start()
                score(chunk, piece, z)
            else:

                def every(block, unused, chunk=chunk, piece=piece):
                    score(chunk, piece, block)
                    return unused

                lax.fori_loop(0, wide, every, 0)

    span = jnp.broadcast_to(span_ref[pl.ds(w, 1), :], (8, span_ref.shape[1]))
    lane = lax.broadcasted_iota(jnp.int32, span.shape, 1)
    row_count = span.shape[1]
    total = scores[z]
    for step in range(1, half):
        source = near(step)
        share_copy(z, source).wait_recv()
        total = total + shares[source]
    for slot in range(half):
        coarse_copy(0, slot).wait_recv()
        total = total + coarse_in[slot].astype(jnp.float32)

    distance = 1
    while distance < min(SPAN_MOST, row_count):
        same = (pltpu.roll(span, distance, 1) == span) & (lane >= distance)
        earlier = jnp.where(same[:1], pltpu.roll(total, distance, 1), total)
        total = jnp.maximum(total, earlier)
        distance *= 2
    last = (pltpu.roll(span, row_count - 1, 1) != span) | (lane == row_count - 1)
    doc_share = peaks_out.shape[1]
    docs = doc_share * narrow
    wanted = lax.broadcasted_iota(jnp.int32, (docs, row_count), 0)
    pick = ((span[:1] == wanted) & last[:1]).astype(jnp.float32)
    peaks = lax.dot_general(
        pick, total, ROW_BY_ROW, precision=HIGHEST, preferred_element_type=jnp.float32
    )
    peaks = jnp.where(jnp.sum(pick, axis=1, keepdims=True) > 0, peaks, LOWEST)
    for index in range(narrow):
        peaks_out[index] = peaks[index * doc_share : (index + 1) * doc_share]
    for step in range(1, narrow):
        peak_copy(other(z, step, narrow), w).start()

    @pl.when(w != z)
    def _():
        peak_copy(z, w).start()

    @pl.when(w == z)
    def _():
        peaks_in[w] = peaks_out[z]

    group_slots = sums.shape[2]
    cands = group_ref.shape[1]
    member = (
        group_ref[...] == lax.broadcasted_iota(jnp.int32, (group_slots, cands), 0)
    ).astype(jnp.float32)
    for step in range(1, wide):
        peak_copy(z, other(w, step, wide)).wait_recv()

    @pl.when(w != z)
    def _():
        peak_copy(z, w).wait_recv()

    doc_peak = peaks_in[0]
    for index in range(1, wide):
        doc_peak = jnp.maximum(doc_peak, peaks_in[index])
    sums[w] = lax.dot_general(
        doc_peak, member, ROW_BY_ROW, precision=HIGHEST, preferred_element_type=jnp.float32
    )
    for step in range(1, wide):
        sum_copy(other(w, step, wide), w).start()
    for step in range(1, wide):
        sum_copy(w, other(w, step, wide)).wait_recv()
    mean = sums[0]
    for index in range(1, wide):
        mean = mean + sums[index]
    out_ref[...] = doc_peak - jnp.dot(
        mean * (1.0 / NBEST), member, precision=HIGHEST, preferred_element_type=jnp.float32
    )

    for chunk in range(chunks):
        for step in range(1, narrow):
            rows_copy(chunk, other(z, step, narrow), z).wait_send()
            for piece in range(pieces_out):
                made_copy(chunk, piece, other(z, step, narrow), z).wait_send()
    for step in range(1, chips):
        there = other(chip, step, chips)
        grad_copy(there, w).wait_send()
        pass_copy(there, there * CORES + core).wait_send()
    own_pass(w).wait_send()
    for step in range(1, narrow):
        peak_copy(other(z, step, narrow), w).wait_send()

    for step in range(1, half):
        share_copy(near(step), z).wait_send()
    for step in range(half):
        coarse_copy(step, lax.rem(z, half)).wait_send()

    @pl.when(w != z)
    def _():
        peak_copy(z, w).wait_send()

    for step in range(1, wide):
        sum_copy(other(w, step, wide), w).wait_send()


def solution(mesh):
    wide, narrow = mesh.shape["wide"], mesh.shape["narrow"]
    assert wide == narrow

    def local(cand_grads, train_feats, span_ids, group_ids, eig_values, input_basis, basis):
        cands, width = cand_grads.shape
        train_rows = train_feats.shape[0]
        peer_rows = train_rows // narrow
        chunks = max(1, peer_rows // 16)
        rows = peer_rows // chunks
        pieces = 2 if width % 512 == 0 else 1
        doc_share = DOCS_DEV * wide // narrow
        group_slots = -(-(cands * wide // NBEST) // 128) * 128
        in_vmem = pl.BlockSpec(memory_space=pltpu.VMEM)
        anywhere = pl.BlockSpec(memory_space=pltpu.HBM)
        dma = pltpu.SemaphoreType.DMA
        turned = pl.pallas_call(
            functools.partial(kernel, chunks),
            out_shape=jax.ShapeDtypeStruct((doc_share, cands), jnp.float32),
            in_specs=[anywhere] * 7,
            out_specs=in_vmem,
            scratch_shapes=[
                pltpu.VMEM((wide, train_rows), jnp.int32),
                pltpu.VMEM((1, cands), jnp.int32),
                pltpu.VMEM(eig_values.shape, jnp.float32),
                pltpu.VMEM(input_basis.shape, jnp.float32),
                pltpu.VMEM(basis.shape, jnp.float32),
                pltpu.VMEM((chunks, narrow, rows, width), jnp.bfloat16),
                pltpu.VMEM((chunks, narrow, rows, width), jnp.bfloat16),
                pltpu.VMEM((chunks, narrow, rows, width), jnp.bfloat16),
                pltpu.VMEM((wide, cands, width), jnp.bfloat16),
                pltpu.VMEM((wide, cands, train_rows), jnp.float32),
                pltpu.VMEM((narrow, cands, train_rows), jnp.float32),
                pltpu.VMEM((chunks, narrow, rows, width), jnp.bfloat16),
                pltpu.VMEM((narrow // 2, cands, train_rows), jnp.bfloat16),
                pltpu.VMEM((narrow // 2, cands, train_rows), jnp.bfloat16),
                pltpu.VMEM((narrow, doc_share, cands), jnp.float32),
                pltpu.VMEM((wide, doc_share, cands), jnp.float32),
                pltpu.VMEM((wide, doc_share, group_slots), jnp.float32),
                dma((chunks, narrow)),
                dma((chunks, narrow)),
                dma((chunks, pieces, narrow)),
                dma((chunks, pieces, narrow)),
                dma((wide // CORES,)),
                dma((wide // CORES,)),
                dma((wide,)),
                dma((narrow,)),
                dma((narrow,)),
                dma((narrow // 2,)),
                dma((narrow // 2,)),
                dma((narrow,)),
                dma((wide,)),
                dma((wide,)),
                dma((wide,)),
                dma((chunks,)),
                dma(()),
                dma((5,)),
            ],
            compiler_params=pltpu.CompilerParams(
                collective_id=0, has_side_effects=True, vmem_limit_bytes=63 * 2**20
            ),
        )(
            train_feats.reshape(chunks, narrow, rows, width),
            cand_grads,
            span_ids.reshape(wide, train_rows),
            group_ids.reshape(1, cands),
            eig_values,
            input_basis,
            basis,
        )
        return turned.T

    return jax.shard_map(
        local,
        mesh=mesh,
        in_specs=(
            P(("parts", "wide"), "narrow"),
            P(("parts", "wide"), "narrow"),
            P("parts"),
            P(("parts", "wide")),
            P(),
            P(),
            P(),
        ),
        out_specs=P(("parts", "wide"), "narrow"),
        check_vma=False,
    )
```

```python
import functools

import jax
import jax.numpy as jnp
from jax import lax
from jax.experimental import pallas as pl
from jax.experimental.pallas import tpu as pltpu
from jax.sharding import PartitionSpec as P

DOCS_DEV = 16
NBEST = 16
SPAN_MOST = 32
CORES = 2
DAMPING = 0.05
LOWEST = -1e30

MESH = pl.DeviceIdType.MESH
HIGHEST = lax.Precision.HIGHEST
ROW_BY_ROW = (((1,), (1,)), ((), ()))


def split(value):
    high = value.astype(jnp.bfloat16)
    return high, (value - high.astype(jnp.float32)).astype(jnp.bfloat16)


def product(left, right):
    return jnp.dot(left, right, preferred_element_type=jnp.float32)


def thirds(value, picks, dimensions):
    high, rest = split(value)
    middle = value - high.astype(jnp.float32)
    low = (middle - rest.astype(jnp.float32)).astype(jnp.bfloat16)
    terms = lax.dot_general(
        jnp.concatenate([high, rest, low], axis=0), picks, dimensions,
        preferred_element_type=jnp.float32,
    )
    count = value.shape[0]
    return terms[:count] + terms[count : 2 * count] + terms[2 * count :]


def stack_rows(pieces):
    if pieces[0].shape[0] % 16:
        joined = jnp.concatenate([piece.astype(jnp.float32) for piece in pieces], axis=0)
        return joined.astype(jnp.bfloat16)
    return jnp.concatenate(pieces, axis=0)


def kernel(
    chunks, t_ref, g_ref, span_hbm, group_hbm, eig_hbm, in_hbm, basis_hbm, out_ref,
    span_ref, group_ref, eig_ref, in_ref, basis_ref, taken, made, held, gathered, scores, shares, low, coarse, coarse_in, peaks_out, peaks_in, sums,
    t_send, t_recv, m_send, m_recv, g_send, g_pass, g_recv, s_send, s_recv, c_send, c_recv,
    p_send, p_recv, q_send, q_recv, t_local, g_local, small,
):
    wide, narrow = lax.axis_size("wide"), lax.axis_size("narrow")
    w, z = lax.axis_index("wide"), lax.axis_index("narrow")
    chips = wide // CORES
    chip, core = w // CORES, lax.rem(w, CORES)
    sibling = chip * CORES + 1 - core
    rows = taken.shape[2]
    local_in = taken.shape[3] // 128
    size = basis_ref.shape[0]
    pieces_out = m_send.shape[1]
    piece_width = taken.shape[3] // pieces_out

    def other(index, step, count):
        return lax.rem(index + step, count)

    def remote(source, target, send, recv, device):
        return pltpu.make_async_remote_copy(
            src_ref=source, dst_ref=target, send_sem=send, recv_sem=recv,
            device_id=device, device_id_type=MESH,
        )

    def rows_copy(chunk, peer, slot):
        return remote(
            t_ref.at[chunk, peer], taken.at[chunk, slot],
            t_send.at[chunk, peer], t_recv.at[chunk, slot], {"narrow": peer},
        )

    def made_copy(chunk, piece, peer, slot):
        columns = pl.ds(piece * piece_width, piece_width)
        return remote(
            made.at[chunk, peer, :, columns], held.at[chunk, slot, :, columns],
            m_send.at[chunk, piece, peer], m_recv.at[chunk, piece, slot], {"narrow": peer},
        )

    def grad_copy(there, slot):
        return remote(
            g_ref, gathered.at[slot], g_send.at[there], g_recv.at[slot],
            {"wide": there * CORES + core},
        )

    def pass_copy(here, slot):
        return remote(
            gathered.at[slot], gathered.at[slot], g_pass.at[here], g_recv.at[slot], {"wide": sibling}
        )

    def own_pass(slot):
        return remote(g_ref, gathered.at[slot], g_pass.at[chip], g_recv.at[slot], {"wide": sibling})

    def share_copy(peer, slot):
        return remote(
            scores.at[peer], shares.at[slot], s_send.at[peer], s_recv.at[slot], {"narrow": peer}
        )

    half = narrow // 2
    near_base = z // half * half
    far_base = half - near_base

    def near(step):
        return near_base + lax.rem(z + step, half)

    def far(step):
        return far_base + lax.rem(z + step, half)

    peers = [far(step) for step in range(half)] + [near(step) for step in range(1, half)]

    def coarse_copy(step, slot):
        return remote(
            coarse.at[step], coarse_in.at[slot], c_send.at[step], c_recv.at[slot],
            {"narrow": far(step)},
        )

    def peak_copy(docs, slot):
        return remote(
            peaks_out.at[docs], peaks_in.at[slot], p_send.at[docs], p_recv.at[slot],
            {"wide": z, "narrow": docs},
        )

    def sum_copy(peer, slot):
        return remote(sums.at[w], sums.at[slot], q_send.at[peer], q_recv.at[slot], {"wide": peer})

    fetches = [
        pltpu.make_async_copy(source, target, small.at[index])
        for index, (source, target) in enumerate(
            (
                (in_hbm, in_ref),
                (basis_hbm, basis_ref),
                (eig_hbm, eig_ref),
                (span_hbm, span_ref),
                (group_hbm, group_ref),
            )
        )
    ]
    barrier = pltpu.get_barrier_semaphore()
    for step in range(1, narrow):
        pl.semaphore_signal(
            barrier, inc=1, device_id={"narrow": other(z, step, narrow)}, device_id_type=MESH
        )
    for step in range(1, wide):
        peer = other(w, step, wide)
        pl.semaphore_signal(barrier, inc=1, device_id={"wide": peer}, device_id_type=MESH)
        pl.semaphore_signal(
            barrier, inc=1, device_id={"wide": peer, "narrow": w}, device_id_type=MESH
        )
    own_rows = [
        pltpu.make_async_copy(t_ref.at[chunk, z], taken.at[chunk, z], t_local.at[chunk])
        for chunk in range(chunks)
    ]
    own_grads = pltpu.make_async_copy(g_ref, gathered.at[w], g_local)
    for copy in own_rows + fetches + [own_grads]:
        copy.start()
    pl.semaphore_wait(barrier, narrow - 1 + wide - 1 + jnp.where(w == z, 0, narrow))

    for chunk in range(chunks):
        for peer in peers:
            rows_copy(chunk, peer, z).start()
        if chunk == 0:
            for step in range(1, chips):
                grad_copy(other(chip, step, chips), w).start()
            own_pass(w).start()

    for fetch in fetches:
        fetch.wait()
    in_basis, out_basis = in_ref[...], basis_ref[...]
    in_high, in_low = split(in_basis)
    inT_high, inT_low = split(in_basis.T)
    out_high, out_low = split(out_basis)
    outT_high, outT_low = split(out_basis.T)
    into = jnp.concatenate([out_high, out_low], axis=1)
    back = jnp.concatenate(
        [
            jnp.concatenate([outT_high, outT_low], axis=1),
            jnp.concatenate([outT_high, jnp.zeros_like(outT_low)], axis=1),
        ],
        axis=0,
    )
    in_into = jnp.concatenate([inT_high, inT_high, inT_low], axis=1)
    in_back = jnp.concatenate([in_high, in_high, in_low], axis=1)
    weight = 1.0 / (eig_ref[...] + DAMPING)

    def mixed(matrix, blocks):
        wide_block = jnp.concatenate(blocks, axis=1)
        high, low = split(wide_block)
        return product(matrix, jnp.concatenate([high, low, high], axis=0))

    def lane_block(value, index):
        return value[:, index * size : (index + 1) * size]

    def precondition(chunk):
        pieces = [
            taken[chunk, source, :, a * size : (a + 1) * size]
            for source in range(narrow)
            for a in range(local_in)
        ]
        both = product(stack_rows(pieces), into)
        left = both[:, :size] + both[:, size:]
        left = jnp.swapaxes(left.reshape(size, rows, size), 0, 1)
        rotated = mixed(in_into, [left[row] for row in range(rows)])
        scaled = jnp.concatenate([lane_block(rotated, row) * weight for row in range(rows)], axis=0)
        both = product(jnp.concatenate(split(scaled), axis=1), back)
        right = both[:, :size] + both[:, size:]
        restored = mixed(in_back, [right[row * size : (row + 1) * size] for row in range(rows)])
        result = jnp.stack([lane_block(restored, row) for row in range(rows)], axis=0)
        exact = jnp.swapaxes(result, 0, 1)
        result = exact.astype(jnp.bfloat16)
        rest = exact - result.astype(jnp.float32)
        for target in range(narrow):
            for a in range(local_in):
                made[chunk, target, :, a * size : (a + 1) * size] = result[target * local_in + a]
            keep = jnp.where(z == target, 1.0, 0.0)
            for a in range(local_in):
                low[chunk, target, :, a * size : (a + 1) * size] = (
                    rest[target * local_in + a] * keep
                ).astype(jnp.bfloat16)

    for chunk in range(chunks):
        own_rows[chunk].wait()
        for step in range(1, narrow):
            rows_copy(chunk, z, other(z, step, narrow)).wait_recv()
        precondition(chunk)
        for piece in range(pieces_out):
            for peer in peers:
                made_copy(chunk, piece, peer, z).start()
        held[chunk, z] = made[chunk, z]

    for step in range(1, chips):
        there = other(chip, step, chips)
        slot = there * CORES + core
        grad_copy(there, slot).wait_recv()
        pass_copy(there, slot).start()
    own_grads.wait()
    for step in range(chips):
        there = other(chip, step, chips)
        pass_copy(there, there * CORES + 1 - core).wait_recv()

    def score(chunk, piece, block):
        width = narrow * rows
        place = (block, slice(None), slice(chunk * width, (chunk + 1) * width))
        columns = slice(piece * piece_width, (piece + 1) * piece_width)
        train = stack_rows(
            [part[chunk, source, :, columns] for part in (held, low) for source in range(narrow)]
        )
        value = lax.dot_general(
            gathered[block, :, columns], train, ROW_BY_ROW, preferred_element_type=jnp.float32
        )
        value = value[:, :width] + value[:, width:]
        scores[place] = value if piece == 0 else scores[place] + value

    for chunk in range(chunks):
        for piece in range(pieces_out):
            for step in range(1, narrow):
                made_copy(chunk, piece, z, other(z, step, narrow)).wait_recv()
            if chunk == chunks - 1 and piece == pieces_out - 1:
                for step in range(half):
                    block = far(step)
                    score(chunk, piece, block)
                    coarse[step] = scores[block].astype(jnp.bfloat16)
                    coarse_copy(step, lax.rem(z, half)).start()
                for step in range(1, half):
                    block = near(step)
                    score(chunk, piece, block)
                    share_copy(block, z).start()
                score(chunk, piece, z)
            else:

                def every(block, unused, chunk=chunk, piece=piece):
                    score(chunk, piece, block)
                    return unused

                lax.fori_loop(0, wide, every, 0)

    for chunk in range(chunks):
        for step in range(1, narrow):
            rows_copy(chunk, other(z, step, narrow), z).wait_send()
            for piece in range(pieces_out):
                made_copy(chunk, piece, other(z, step, narrow), z).wait_send()
    for step in range(1, chips):
        there = other(chip, step, chips)
        grad_copy(there, w).wait_send()
        pass_copy(there, there * CORES + core).wait_send()
    own_pass(w).wait_send()
    span = jnp.broadcast_to(span_ref[pl.ds(w, 1), :], (8, span_ref.shape[1]))
    lane = lax.broadcasted_iota(jnp.int32, span.shape, 1)
    row_count = span.shape[1]
    total = scores[z]
    for step in range(1, half):
        source = near(step)
        share_copy(z, source).wait_recv()
        total = total + shares[source]
    for slot in range(half):
        coarse_copy(0, slot).wait_recv()
        total = total + coarse_in[slot].astype(jnp.float32)

    distance = 1
    while distance < min(SPAN_MOST, row_count):
        same = (pltpu.roll(span, distance, 1) == span) & (lane >= distance)
        earlier = jnp.where(same[:1], pltpu.roll(total, distance, 1), total)
        total = jnp.maximum(total, earlier)
        distance *= 2
    last = (pltpu.roll(span, row_count - 1, 1) != span) | (lane == row_count - 1)
    doc_share = peaks_out.shape[1]
    docs = doc_share * narrow
    wanted = lax.broadcasted_iota(jnp.int32, (docs, row_count), 0)
    pick = ((span[:1] == wanted) & last[:1]).astype(jnp.float32)
    peaks = lax.dot_general(
        pick, total, ROW_BY_ROW, precision=HIGHEST, preferred_element_type=jnp.float32
    )
    peaks = jnp.where(jnp.sum(pick, axis=1, keepdims=True) > 0, peaks, LOWEST)
    for index in range(narrow):
        peaks_out[index] = peaks[index * doc_share : (index + 1) * doc_share]
    for step in range(1, narrow):
        peak_copy(other(z, step, narrow), w).start()

    @pl.when(w != z)
    def _():
        peak_copy(z, w).start()

    @pl.when(w == z)
    def _():
        peaks_in[w] = peaks_out[z]

    for step in range(1, half):
        share_copy(near(step), z).wait_send()
    for step in range(half):
        coarse_copy(step, lax.rem(z, half)).wait_send()
    group_slots = sums.shape[2]
    cands = group_ref.shape[1]
    member = (
        group_ref[...] == lax.broadcasted_iota(jnp.int32, (group_slots, cands), 0)
    ).astype(jnp.bfloat16)
    for step in range(1, wide):
        peak_copy(z, other(w, step, wide)).wait_recv()

    @pl.when(w != z)
    def _():
        peak_copy(z, w).wait_recv()

    doc_peak = peaks_in[0]
    for index in range(1, wide):
        doc_peak = jnp.maximum(doc_peak, peaks_in[index])
    sums[w] = thirds(doc_peak, member, ROW_BY_ROW)
    for step in range(1, wide):
        sum_copy(other(w, step, wide), w).start()
    for step in range(1, wide):
        sum_copy(w, other(w, step, wide)).wait_recv()
    mean = sums[0]
    for index in range(1, wide):
        mean = mean + sums[index]
    out_ref[...] = doc_peak - thirds(mean * (1.0 / NBEST), member, (((1,), (0,)), ((), ())))

    for step in range(1, narrow):
        peak_copy(other(z, step, narrow), w).wait_send()


    @pl.when(w != z)
    def _():
        peak_copy(z, w).wait_send()

    for step in range(1, wide):
        sum_copy(other(w, step, wide), w).wait_send()


def solution(mesh):
    wide, narrow = mesh.shape["wide"], mesh.shape["narrow"]
    assert wide == narrow

    def local(cand_grads, train_feats, span_ids, group_ids, eig_values, input_basis, basis):
        cands, width = cand_grads.shape
        train_rows = train_feats.shape[0]
        peer_rows = train_rows // narrow
        chunks = max(1, peer_rows // 16)
        rows = peer_rows // chunks
        pieces = 2 if width % 512 == 0 else 1
        doc_share = DOCS_DEV * wide // narrow
        group_slots = -(-(cands * wide // NBEST) // 128) * 128
        in_vmem = pl.BlockSpec(memory_space=pltpu.VMEM)
        anywhere = pl.BlockSpec(memory_space=pltpu.HBM)
        dma = pltpu.SemaphoreType.DMA
        turned = pl.pallas_call(
            functools.partial(kernel, chunks),
            out_shape=jax.ShapeDtypeStruct((doc_share, cands), jnp.float32),
            in_specs=[anywhere] * 7,
            out_specs=in_vmem,
            scratch_shapes=[
                pltpu.VMEM((wide, train_rows), jnp.int32),
                pltpu.VMEM((1, cands), jnp.int32),
                pltpu.VMEM(eig_values.shape, jnp.float32),
                pltpu.VMEM(input_basis.shape, jnp.float32),
                pltpu.VMEM(basis.shape, jnp.float32),
                pltpu.VMEM((chunks, narrow, rows, width), jnp.bfloat16),
                pltpu.VMEM((chunks, narrow, rows, width), jnp.bfloat16),
                pltpu.VMEM((chunks, narrow, rows, width), jnp.bfloat16),
                pltpu.VMEM((wide, cands, width), jnp.bfloat16),
                pltpu.VMEM((wide, cands, train_rows), jnp.float32),
                pltpu.VMEM((narrow, cands, train_rows), jnp.float32),
                pltpu.VMEM((chunks, narrow, rows, width), jnp.bfloat16),
                pltpu.VMEM((narrow // 2, cands, train_rows), jnp.bfloat16),
                pltpu.VMEM((narrow // 2, cands, train_rows), jnp.bfloat16),
                pltpu.VMEM((narrow, doc_share, cands), jnp.float32),
                pltpu.VMEM((wide, doc_share, cands), jnp.float32),
                pltpu.VMEM((wide, doc_share, group_slots), jnp.float32),
                dma((chunks, narrow)),
                dma((chunks, narrow)),
                dma((chunks, pieces, narrow)),
                dma((chunks, pieces, narrow)),
                dma((wide // CORES,)),
                dma((wide // CORES,)),
                dma((wide,)),
                dma((narrow,)),
                dma((narrow,)),
                dma((narrow // 2,)),
                dma((narrow // 2,)),
                dma((narrow,)),
                dma((wide,)),
                dma((wide,)),
                dma((wide,)),
                dma((chunks,)),
                dma(()),
                dma((5,)),
            ],
            compiler_params=pltpu.CompilerParams(
                collective_id=0, has_side_effects=True, vmem_limit_bytes=63 * 2**20
            ),
        )(
            train_feats.reshape(chunks, narrow, rows, width),
            cand_grads,
            span_ids.reshape(wide, train_rows),
            group_ids.reshape(1, cands),
            eig_values,
            input_basis,
            basis,
        )
        return turned.T

    return jax.shard_map(
        local,
        mesh=mesh,
        in_specs=(
            P(("parts", "wide"), "narrow"),
            P(("parts", "wide"), "narrow"),
            P("parts"),
            P(("parts", "wide")),
            P(),
            P(),
            P(),
        ),
        out_specs=P(("parts", "wide"), "narrow"),
        check_vma=False,
    )
```
